256 devices in a mesh: row: 16 (over z, core), col: 16 (over x, y).
Axes of the slice: x: 4, y: 4, z: 8, core: 2. Of those that a mesh axis runs over, the one named last changes fastest.
Arguments:
- tokens: bfloat16 [1024, 5120], P('col', 'row'), may hold values from -6 to 6
- up_weight: bfloat16 [5120, 20480], P('row', 'col'), may hold values from -0.078125 to 0.078125
- down_weight: bfloat16 [20480, 5120], P('col', 'row'), may hold values from -0.0390625 to 0.0390625
- cotangent: bfloat16 [1024, 5120], P('col', 'row'), may hold values from -6 to 6
Outputs:
- mixed: bfloat16 [1024, 5120], P('col', 'row')
- grad_tokens: bfloat16 [1024, 5120], P('col', 'row')
- grad_up: float32 [5120, 20480], P('row', 'col')
- grad_down: float32 [20480, 5120], P('col', 'row')
The draws below stay inside these ranges and needn't reach their ends.
All inputs are finite; a program needn't handle non-finite values.
Results may differ from the reference program's by a relative error of at most 0.0062.
Values may be sent and summed in bfloat16 or wider, within the bound.
No kernel may reach another device: no remote copies, remote signals or barrier semaphores. Data moves between devices by JAX's collectives and lax.ppermute only.
A program may use at most 128 MiB of HBM per device.

```python
import math
import jax
import jax.numpy as jnp
from jax import lax

D = 5120
F = 20480
TOKENS = 1024
N_ROW = 16


def levels(stream_key, dims, cuts, low, top_value):
    loudness = 1.0
    for axis_at, parts in cuts:
        draws = jax.random.uniform(jax.random.fold_in(jax.random.fold_in(stream_key, 6), axis_at), (parts,), jnp.float32, low / len(cuts), top_value / len(cuts))
        loudness = loudness * jnp.repeat(jnp.exp(draws), dims[axis_at] // parts).reshape((-1,) + (1,) * (len(dims) - 1 - axis_at))
    return loudness


def scatter_about(rng, shape, scale, limit, cuts=(), dtype=jnp.bfloat16):
    values = jax.random.normal(rng, shape, jnp.float32) * scale
    if len(cuts) > 0:
        values = levels(rng, shape, cuts, -0.22, 0.18) * values
    return jnp.clip(values, min=-limit, max=limit).astype(dtype)


def setup_inputs(seed: int = 0) -> dict:
    seeds = jax.random.split(jax.random.key(seed), 5)
    return {
        "tokens": scatter_about(seeds[0], (TOKENS, D), 1.0, 6.0, ((0, 16), (1, 16))),
        "up_weight": scatter_about(seeds[1], (D, F), D ** -0.5, 0.078125, ((0, 16), (1, 16))),
        "down_weight": scatter_about(seeds[2], (F, D), F ** -0.5, 0.0390625, ((0, 16), (1, 16))),
        "cotangent": scatter_about(seeds[3], (TOKENS, D), 1.0, 6.0, ((0, 16), (1, 16))),
    }


root_coef = math.sqrt(2.0 / math.pi)

def gelu_tanh(value):
    inner = root_coef * (value + 0.044715 * value * value * value)
    return 0.5 * value * (1.0 + jnp.tanh(inner))

def gelu_slope(value):
    inner = root_coef * (value + 0.044715 * value * value * value)
    tanh_val = jnp.tanh(inner)
    return 0.5 * (1.0 + tanh_val) + 0.5 * value * (1.0 - tanh_val * tanh_val) * root_coef * (1.0 + 3.0 * 0.044715 * value * value)

def rounded_blocks(left, right, count):
    width = left.shape[1] // count
    lefts = left.reshape(left.shape[0], count, width).transpose(1, 0, 2)
    rights = right.reshape(count, width, right.shape[1])

    def add_block(total, pair):
        piece = jnp.dot(pair[0], pair[1], preferred_element_type=jnp.float32).astype(jnp.bfloat16)
        piece = lax.optimization_barrier(piece)
        return (total + piece.astype(jnp.float32), None)
    start = jnp.zeros((left.shape[0], right.shape[1]), jnp.float32)
    total, _ = lax.scan(add_block, start, (lefts, rights))
    return total

def reference(tokens, up_weight, down_weight, cotangent):
    pre_act = rounded_blocks(tokens, up_weight, N_ROW)
    activ = gelu_tanh(pre_act).astype(jnp.bfloat16)
    mixed = jnp.dot(activ, down_weight, preferred_element_type=jnp.float32).astype(jnp.bfloat16)
    grad_act = rounded_blocks(cotangent, down_weight.T, N_ROW)
    grad_pre = (grad_act * gelu_slope(pre_act)).astype(jnp.bfloat16)
    grad_tokens = jnp.dot(grad_pre, up_weight.T, preferred_element_type=jnp.float32).astype(jnp.bfloat16)
    scale = 1.0 / math.sqrt(TOKENS)
    grad_up = jnp.dot(tokens.T, grad_pre, preferred_element_type=jnp.float32) * scale
    grad_down = jnp.dot(activ.T, cotangent, preferred_element_type=jnp.float32) * scale
    return (mixed, grad_tokens, grad_up, grad_down)
```

```python
import functools
import math

import jax
import jax.numpy as jnp
from jax import lax
from jax.experimental import pallas as pl
from jax.experimental.pallas import tpu as pltpu
from jax.sharding import PartitionSpec as P

root_coef = math.sqrt(2.0 / math.pi)
f32 = jnp.float32
bf16 = jnp.bfloat16

NZ = 8
NX = 4
NY = 4


def gelu_and_slope(value):
    inner = root_coef * (value + 0.044715 * value * value * value)
    tanh_val = jnp.tanh(inner)
    act = 0.5 * value * (1.0 + tanh_val)
    slope = 0.5 * (1.0 + tanh_val) + 0.5 * value * (1.0 - tanh_val * tanh_val) * root_coef * (
        1.0 + 3.0 * 0.044715 * value * value
    )
    return act, slope


def pairs(axis, first):
    out = []
    for z in range(NZ):
        for core in range(2):
            for x in range(NX):
                for y in range(NY):
                    at = {"z": z, "x": x, "y": y}
                    size = {"z": NZ, "x": NX, "y": NY}[axis]
                    step = 1 if (at[axis] + core) % 2 == 0 else -1
                    at[axis] = (at[axis] + (step if first else -step)) % size
                    src = (z * 2 + core) * 16 + x * 4 + y
                    dst = (at["z"] * 2 + core) * 16 + at["x"] * 4 + at["y"]
                    out.append((src, dst))
    return out


PERMS = {(axis, first): pairs(axis, first) for axis in "xyz" for first in (True, False)}


def swap1(axis, value):
    return lax.ppermute(value, ("row", "col"), PERMS[(axis, True)])


def swap2(axis, value):
    return lax.ppermute(value, ("row", "col"), PERMS[(axis, False)])


def core_swap(value):
    return lax.ppermute(value, "row", [(r, r ^ 1) for r in range(2 * NZ)])


def rotate_kernel(zs_ref, in_ref, out_ref, *, to_rel):
    z = zs_ref[0]
    s = zs_ref[1]
    for k in range(NZ):
        place = (z + s * k + 16) & (NZ - 1)
        if to_rel:
            out_ref[k] = in_ref[place]
        else:
            out_ref[place] = in_ref[k]


def rotate(value, zs, to_rel):
    return pl.pallas_call(
        functools.partial(rotate_kernel, to_rel=to_rel),
        out_shape=jax.ShapeDtypeStruct(value.shape, value.dtype),
        in_specs=[
            pl.BlockSpec(memory_space=pltpu.SMEM),
            pl.BlockSpec(memory_space=pltpu.VMEM),
        ],
        out_specs=pl.BlockSpec(memory_space=pltpu.VMEM),
    )(zs, value)


def gather_tokens(block, order):
    held = block[None]
    for axis in order:
        held = jnp.concatenate([held, swap1(axis, held)], axis=0)
        held = jnp.concatenate([held, swap2(axis, held)], axis=0)
    return held


def reduce_z(part):
    half = part[0].shape[0] // 2
    first = swap1("z", part[4][:half].astype(bf16))
    second = swap2("z", part[4][half:].astype(bf16))
    plus = jnp.concatenate([part[3][:half], part[3][half:] + second.astype(f32)], axis=0)
    minus = jnp.concatenate([part[5][:half] + first.astype(f32), part[5][half:]], axis=0)
    for k in (2, 1, 0):
        first = swap1("z", plus.astype(bf16))
        second = swap2("z", minus.astype(bf16))
        if k:
            plus = part[k] + second.astype(f32)
            minus = part[8 - k] + first.astype(f32)
    return part[0] + first.astype(f32) + second.astype(f32)


def gather_z(own):
    got = {0: own}
    got[1] = swap1("z", own)
    got[7] = swap2("z", own)
    for k in (2, 3):
        got[k] = swap1("z", got[9 - k])
        got[8 - k] = swap2("z", got[k - 1])
    half = own.shape[0] // 2
    front = swap2("z", got[3][:half])
    back = swap1("z", got[5][half:])
    got[4] = jnp.concatenate([front, back], axis=0)
    return jnp.concatenate([got[k] for k in range(8)], axis=0)


def reduce_tokens(part, order):
    for axis in order:
        if axis == "y":
            keep, away = part[:, :2], part[:, 2:]
            part = keep + swap2("y", away.astype(bf16)).astype(f32)
            keep, away = part[:, :1], part[:, 1:]
            part = keep + swap1("y", away.astype(bf16)).astype(f32)
        else:
            keep, away = part[:, :, :2], part[:, :, 2:]
            part = keep + swap2("x", away.astype(bf16)).astype(f32)
            keep, away = part[:, :, :1], part[:, :, 1:]
            part = keep + swap1("x", away.astype(bf16)).astype(f32)
    return part[:, 0, 0]


def contract_last(left, right):
    return lax.dot_general(left, right, (((1,), (1,)), ((), ())), preferred_element_type=f32)


def contract_first(left, right):
    return lax.dot_general(left, right, (((0,), (0,)), ((), ())), preferred_element_type=f32)


def local(tokens, up_weight, down_weight, cotangent):
    row = lax.axis_index("row")
    z = row // 2
    core = row % 2
    s = 1 - 2 * ((z + core) % 2)
    zs = jnp.stack([z, s]).astype(jnp.int32)
    zs_sib = jnp.stack([z, -s]).astype(jnp.int32)
    width = tokens.shape[1]
    hid = up_weight.shape[1] // 2

    up_own = lax.dynamic_slice_in_dim(up_weight, core * hid, hid, 1)
    up_sib = core_swap(lax.dynamic_slice_in_dim(up_weight, (1 - core) * hid, hid, 1))
    down_own = lax.dynamic_slice_in_dim(down_weight, core * hid, hid, 0)
    down_sib = core_swap(lax.dynamic_slice_in_dim(down_weight, (1 - core) * hid, hid, 0))
    up = jnp.concatenate([up_own, up_sib], axis=0)
    down = jnp.concatenate([down_own, down_sib], axis=1)

    def start(value):
        own = value.reshape(8, 8, width)
        mine = rotate(own, zs, True)
        sib = core_swap(rotate(own, zs_sib, True))
        return jnp.concatenate([mine, sib], axis=-1).reshape(64, 2 * width)

    tok16 = gather_tokens(start(tokens), "xy").reshape(4, 4, 8, 8, 2 * width)
    cot16 = gather_tokens(start(cotangent), "yx").reshape(4, 4, 8, 8, 2 * width)
    tok = tok16.transpose(2, 0, 1, 3, 4).reshape(1024, 2 * width)
    cot = cot16.transpose(2, 1, 0, 3, 4).reshape(1024, 2 * width)

    pre_part = jnp.dot(tok, up, preferred_element_type=f32).reshape(8, 128, hid)
    dact_part = contract_last(cot, down).reshape(8, 128, hid)
    pre = reduce_z(pre_part)
    dact = reduce_z(dact_part)
    act, slope = gelu_and_slope(pre)
    act_all = gather_z(act.astype(bf16))
    dpre_all = gather_z((dact * slope).astype(bf16))

    mixed_part = jnp.dot(act_all, down, preferred_element_type=f32)
    gtok_part = contract_last(dpre_all, up)
    mixed = reduce_tokens(mixed_part.reshape(8, 4, 4, 8, 2 * width), "yx")
    gtok = reduce_tokens(gtok_part.reshape(8, 4, 4, 8, 2 * width), "xy")

    def finish(value):
        value = rotate(value, zs, False).reshape(64, 2 * width)
        return (value[:, :width] + core_swap(value[:, width:])).astype(bf16)

    scale = 1.0 / math.sqrt(1024)
    grad_up = contract_first(tok, dpre_all) * scale
    grad_down = contract_first(act_all, cot) * scale
    gu_own, gu_sib = grad_up[:width], core_swap(grad_up[width:])
    gd_own, gd_sib = grad_down[:, :width], core_swap(grad_down[:, width:])
    low = core == 0
    gu = jnp.concatenate([jnp.where(low, gu_own, gu_sib), jnp.where(low, gu_sib, gu_own)], axis=1)
    gd = jnp.concatenate([jnp.where(low, gd_own, gd_sib), jnp.where(low, gd_sib, gd_own)], axis=0)
    return (finish(mixed), finish(gtok), gu, gd)


def solution(mesh):
    placed = (P("col", "row"), P("row", "col"), P("col", "row"), P("col", "row"))
    return jax.shard_map(
        local,
        mesh=mesh,
        in_specs=placed,
        out_specs=(P("col", "row"), P("col", "row"), P("row", "col"), P("col", "row")),
        check_vma=False,
    )
```

```python
import functools
import math

import jax
import jax.numpy as jnp
from jax import lax
from jax.experimental import pallas as pl
from jax.experimental.pallas import tpu as pltpu
from jax.sharding import PartitionSpec as P

root_coef = math.sqrt(2.0 / math.pi)
f32 = jnp.float32
bf16 = jnp.bfloat16

NZ = 8
NX = 4
NY = 4


def gelu_and_slope(value):
    inner = root_coef * (value + 0.044715 * value * value * value)
    tanh_val = jnp.tanh(inner)
    act = 0.5 * value * (1.0 + tanh_val)
    slope = 0.5 * (1.0 + tanh_val) + 0.5 * value * (1.0 - tanh_val * tanh_val) * root_coef * (
        1.0 + 3.0 * 0.044715 * value * value
    )
    return act, slope


def pairs(axis, first):
    out = []
    for z in range(NZ):
        for core in range(2):
            for x in range(NX):
                for y in range(NY):
                    at = {"z": z, "x": x, "y": y}
                    size = {"z": NZ, "x": NX, "y": NY}[axis]
                    step = 1 if (at[axis] + core) % 2 == 0 else -1
                    at[axis] = (at[axis] + (step if first else -step)) % size
                    src = (z * 2 + core) * 16 + x * 4 + y
                    dst = (at["z"] * 2 + core) * 16 + at["x"] * 4 + at["y"]
                    out.append((src, dst))
    return out


PERMS = {(axis, first): pairs(axis, first) for axis in "xyz" for first in (True, False)}


def swap1(axis, value):
    return lax.ppermute(value, ("row", "col"), PERMS[(axis, True)])


def swap2(axis, value):
    return lax.ppermute(value, ("row", "col"), PERMS[(axis, False)])


def core_swap(value):
    return lax.ppermute(value, "row", [(r, r ^ 1) for r in range(2 * NZ)])


def place_of():
    row = lax.axis_index("row")
    z = row // 2
    s = 1 - 2 * ((z + row) & 1)
    return z, s


def arrange_kernel(tok_ref, cot_ref, tok_out, cot_out):
    z, s = place_of()
    for k in range(NZ):
        at = (z + s * k + 16) & (NZ - 1)
        tok_out[k] = tok_ref[at]
        cot_out[k] = cot_ref[at]


def finish_kernel(mix_ref, gtok_ref, mix_out, gtok_out):
    z, s = place_of()
    for k in range(NZ):
        at = (z + s * k + 16) & (NZ - 1)
        mix_out[at] = mix_ref[k].astype(mix_out.dtype)
        gtok_out[at] = gtok_ref[k].astype(gtok_out.dtype)


FLIP = (0, 2, 1, 3)


def parts_kernel(own_ref, sib_ref, wown_ref, wsib_ref, part_ref, town_ref, tsib_ref, *, order, row):
    rows = pl.ds(row, town_ref.shape[-1])
    for k in range(NZ):
        own, sib = [], []
        for y in range(NY):
            for x in range(NX):
                i, j = (y, x) if order == "xy" else (x, y)
                own.append(own_ref[i, j, k].astype(f32))
                sib.append(sib_ref[FLIP[i], FLIP[j], (NZ - k) % NZ].astype(f32))
        own = jnp.concatenate(own, axis=0).astype(bf16)
        sib = jnp.concatenate(sib, axis=0).astype(bf16)
        town_ref[k] = own
        tsib_ref[k] = sib
        part_ref[k] = jnp.dot(own, wown_ref[rows], preferred_element_type=f32) + jnp.dot(
            sib, wsib_ref[rows], preferred_element_type=f32
        )


def outputs_kernel(*refs):
    acts, dpres = refs[:NZ], refs[NZ : 2 * NZ]
    wown_ref, wsib_ref, mo_ref, ms_ref, go_ref, gs_ref = refs[2 * NZ :]
    width = mo_ref.shape[-1]
    up = pl.ds(0, width)
    down = pl.ds(width, width)
    for k in range(NZ):
        act, dpre = acts[k][...], dpres[k][...]
        mo = contract_last(act, wown_ref[down])
        ms = contract_last(act, wsib_ref[down])
        go = contract_last(dpre, wown_ref[up])
        gs = contract_last(dpre, wsib_ref[up])
        for y in range(NY):
            for x in range(NX):
                at = 8 * (y * NX + x)
                mo_ref[y, x, k] = mo[at : at + 8]
                ms_ref[FLIP[y], FLIP[x], (NZ - k) % NZ] = ms[at : at + 8].astype(bf16)
                go_ref[x, y, k] = go[at : at + 8]
                gs_ref[FLIP[x], FLIP[y], (NZ - k) % NZ] = gs[at : at + 8].astype(bf16)


def grads_kernel(*refs):
    acts, dpres = refs[:NZ], refs[NZ : 2 * NZ]
    town_ref, tsib_ref, cown_ref, csib_ref, own_ref, sib_ref, act_ref, dpre_ref = refs[2 * NZ :]
    for k in range(NZ):
        act_ref[128 * k : 128 * k + 128] = acts[k][...]
        dpre_ref[128 * k : 128 * k + 128] = dpres[k][...]
    scale = 1.0 / math.sqrt(1024)
    own_ref[0] = contract_first(town_ref[...], dpre_ref[...]) * scale
    sib_ref[0] = contract_first(tsib_ref[...], dpre_ref[...]) * scale
    own_ref[1] = contract_first(cown_ref[...], act_ref[...]) * scale
    sib_ref[1] = contract_first(csib_ref[...], act_ref[...]) * scale


def place_kernel(own_ref, sib_ref, up_ref, down_ref, sems):
    core = lax.axis_index("row") & 1
    hid = own_ref.shape[2]
    copies = []
    for i, out in enumerate((up_ref, down_ref)):
        for j, src in enumerate((own_ref, sib_ref)):
            at = pl.multiple_of((core if j == 0 else 1 - core) * hid, 128)
            copies.append(
                pltpu.make_async_copy(src.at[i], out.at[:, pl.ds(at, hid)], sems.at[2 * i + j])
            )
    for copy in copies:
        copy.start()
    for copy in copies:
        copy.wait()


VMEM = pl.BlockSpec(memory_space=pltpu.VMEM)


def call(kernel, outs, *args, scratch=(), flops=0):
    return pl.pallas_call(
        kernel,
        out_shape=[jax.ShapeDtypeStruct(shape, dtype) for shape, dtype in outs],
        in_specs=[VMEM] * len(args),
        out_specs=[VMEM] * len(outs),
        scratch_shapes=list(scratch),
        compiler_params=pltpu.CompilerParams(vmem_limit_bytes=16 * 1024 * 1024),
        cost_estimate=pl.CostEstimate(flops=flops, bytes_accessed=4 << 20, transcendentals=0),
    )(*args)


def gather_tokens(block, order):
    held = block[None]
    for axis in order:
        held = jnp.concatenate([held, swap1(axis, held)], axis=0)
        held = jnp.concatenate([held, swap2(axis, held)], axis=0)
    return held


def after(values, *earlier):
    held = lax.optimization_barrier((values, earlier))
    return held[0]


def reduce_z(parts):
    half = parts[0].shape[1] // 2
    sums, moving, last = [], [], ()
    for part in parts:
        sent = after((part[4][:half].astype(bf16), part[4][half:].astype(bf16)), *last)
        last = sent
        moving.append([swap1("z", sent[0]), swap2("z", sent[1])])
    for k in (3, 2, 1):
        for i, part in enumerate(parts):
            first, second = moving[i]
            second = after(second, *last).astype(f32)
            if k == 3:
                plus = jnp.concatenate([part[3][:half], part[3][half:] + second], axis=0)
            else:
                plus = part[k] + second
            plus = plus.astype(bf16)
            first = after(first, plus).astype(f32)
            if k == 3:
                minus = jnp.concatenate([part[5][:half] + first, part[5][half:]], axis=0)
            else:
                minus = part[8 - k] + first
            minus = minus.astype(bf16)
            last = (minus,)
            moving[i] = [swap1("z", plus), swap2("z", minus)]
    for i, part in enumerate(parts):
        first, second = after(tuple(moving[i]), *last)
        sums.append(part[0] + first.astype(f32) + second.astype(f32))
        last = (sums[-1],)
    return sums


def gather_z(owns):
    half = owns[0].shape[0] // 2
    gots = []
    for own in owns:
        gots.append({0: own, 1: swap1("z", own), 7: swap2("z", own)})
    for k in (2, 3):
        for got in gots:
            got[k] = swap1("z", got[9 - k])
            got[8 - k] = swap2("z", got[k - 1])
    for got in gots:
        front = swap2("z", got[3][:half])
        back = swap1("z", got[5][half:])
        got[4] = jnp.concatenate([front, back], axis=0)
    return [[got[k] for k in range(8)] for got in gots]


def reduce_tokens(part, order):
    one, two = order
    part = part[:2] + swap2(one, part[2:].astype(bf16)).astype(f32)
    part = part[0] + swap1(one, part[1].astype(bf16)).astype(f32)
    part = part[:2] + swap2(two, part[2:].astype(bf16)).astype(f32)
    return part[0] + swap1(two, part[1].astype(bf16)).astype(f32)


def contract_last(left, right):
    return lax.dot_general(left, right, (((1,), (1,)), ((), ())), preferred_element_type=f32)


def contract_first(left, right):
    return lax.dot_general(left, right, (((0,), (0,)), ((), ())), preferred_element_type=f32)


def local(tokens, up_weight, down_weight, cotangent):
    core = lax.axis_index("row") % 2
    width = tokens.shape[1]
    hid = up_weight.shape[1] // 2

    tok0, cot0 = call(
        arrange_kernel,
        [((8, 8, width), bf16)] * 2,
        tokens.reshape(8, 8, width),
        cotangent.reshape(8, 8, width),
    )
    tok16 = gather_tokens(tok0.reshape(64, width), "xy").reshape(4, 4, 8, 8, width)
    cot16 = gather_tokens(cot0.reshape(64, width), "yx").reshape(4, 4, 8, 8, width)

    weights = jnp.concatenate([up_weight, down_weight.T], axis=0)
    wown = lax.dynamic_slice_in_dim(weights, core * hid, hid, 1)
    wsib = core_swap(lax.dynamic_slice_in_dim(weights, (1 - core) * hid, hid, 1))

    def parts(mine, order, row):
        out = call(
            functools.partial(parts_kernel, order=order, row=row),
            [((8, 128, hid), f32), ((8, 128, width), bf16), ((8, 128, width), bf16)],
            mine,
            core_swap(mine),
            wown,
            wsib,
            flops=2 * 1024 * hid * 2 * width,
        )
        return out[0], out[1].reshape(1024, width), out[2].reshape(1024, width)

    pre_part, town, tsib = parts(tok16, "xy", 0)
    dact_part, cown, csib = parts(cot16, "yx", width)
    pre, dact = reduce_z([pre_part, dact_part])
    act, slope = gelu_and_slope(pre)
    acts, dpres = gather_z([act.astype(bf16), (dact * slope).astype(bf16)])

    mixed, mixed_sib, gtok, gtok_sib = call(
        outputs_kernel,
        [((4, 4, 8, 8, width), f32), ((4, 4, 8, 8, width), bf16)] * 2,
        *acts,
        *dpres,
        wown,
        wsib,
        flops=2 * 2 * 1024 * hid * 2 * width,
    )
    grad_own, grad_sib = call(
        grads_kernel,
        [((2, width, hid), f32)] * 2,
        *acts,
        *dpres,
        town,
        tsib,
        cown,
        csib,
        scratch=[pltpu.VMEM((1024, hid), bf16)] * 2,
        flops=2 * 2 * 1024 * hid * 2 * width,
    )
    mixed = reduce_tokens(mixed + core_swap(mixed_sib).astype(f32), "yx")
    gtok = reduce_tokens(gtok + core_swap(gtok_sib).astype(f32), "xy")
    mixed, gtok = call(finish_kernel, [((8, 8, width), bf16)] * 2, mixed, gtok)
    any_space = pl.BlockSpec(memory_space=pl.ANY)
    gu, gd = pl.pallas_call(
        place_kernel,
        out_shape=[jax.ShapeDtypeStruct((width, 2 * hid), f32)] * 2,
        in_specs=[VMEM] * 2,
        out_specs=[any_space] * 2,
        scratch_shapes=[pltpu.SemaphoreType.DMA((4,))],
    )(grad_own, core_swap(grad_sib))
    return (mixed.reshape(64, width), gtok.reshape(64, width), gu, gd.T)


def solution(mesh):
    placed = (P("col", "row"), P("row", "col"), P("col", "row"), P("col", "row"))
    return jax.shard_map(
        local,
        mesh=mesh,
        in_specs=placed,
        out_specs=(P("col", "row"), P("col", "row"), P("row", "col"), P("col", "row")),
        check_vma=False,
    )
```

```python
import functools
import math

import jax
import jax.numpy as jnp
from jax import lax
from jax.experimental import pallas as pl
from jax.experimental.pallas import tpu as pltpu
from jax.sharding import PartitionSpec as P

root_coef = math.sqrt(2.0 / math.pi)
f32 = jnp.float32
bf16 = jnp.bfloat16

NZ = 8
NX = 4
NY = 4


def gelu_and_slope(value):
    inner = root_coef * (value + 0.044715 * value * value * value)
    tanh_val = jnp.tanh(inner)
    act = 0.5 * value * (1.0 + tanh_val)
    slope = 0.5 * (1.0 + tanh_val) + 0.5 * value * (1.0 - tanh_val * tanh_val) * root_coef * (
        1.0 + 3.0 * 0.044715 * value * value
    )
    return act, slope


def pairs(axis, which):
    out = []
    size = {"z": NZ, "x": NX, "y": NY}[axis]
    for z in range(NZ):
        for core in range(2):
            for x in range(NX):
                for y in range(NY):
                    at = {"z": z, "x": x, "y": y}
                    step = 1 if (at[axis] + core) % 2 == 0 else -1
                    at[axis] = (at[axis] + {1: step, 2: -step, 3: 2}[which]) % size
                    src = (z * 2 + core) * 16 + x * 4 + y
                    dst = (at["z"] * 2 + core) * 16 + at["x"] * 4 + at["y"]
                    out.append((src, dst))
    return out


PERMS = {
    (axis, which): pairs(axis, which) for axis in "xyz" for which in (1, 2, 3) if axis + str(which) != "z3"
}


def swap(axis, which, value):
    return lax.ppermute(value, ("row", "col"), PERMS[(axis, which)])


def swap1(axis, value):
    return swap(axis, 1, value)


def swap2(axis, value):
    return swap(axis, 2, value)


def core_swap(value):
    return lax.ppermute(value, "row", [(r, r ^ 1) for r in range(2 * NZ)])


def place_of():
    row = lax.axis_index("row")
    z = row // 2
    s = 1 - 2 * ((z + row) & 1)
    return z, s


FLIP = (0, 2, 1, 3)


def finish_kernel(own_ref, one_ref, two_ref, three_ref, mix_ref, gtok_ref):
    for i, out in enumerate((mix_ref, gtok_ref)):
        total = own_ref[i]
        for ref in (one_ref, two_ref, three_ref):
            total += ref[i].astype(f32)
        out[...] = total.astype(out.dtype)


def parts_kernel(own_ref, sib_ref, wown_ref, wsib_ref, part_ref, town_ref, tsib_ref, *, row):
    z, s = place_of()
    rows = pl.ds(row, town_ref.shape[-1])
    for k in range(NZ):
        at = (z + s * k + 16) & (NZ - 1)
        own, sib = [], []
        for y in range(NY):
            for x in range(NX):
                own.append(own_ref[y, x, at].astype(f32))
                sib.append(sib_ref[FLIP[y], FLIP[x], at].astype(f32))
        own = jnp.concatenate(own, axis=0).astype(bf16)
        sib = jnp.concatenate(sib, axis=0).astype(bf16)
        town_ref[k] = own
        tsib_ref[k] = sib
        part_ref[k] = jnp.dot(own, wown_ref[rows], preferred_element_type=f32) + jnp.dot(
            sib, wsib_ref[rows], preferred_element_type=f32
        )


def outputs_kernel(*refs, ks):
    count = len(ks)
    wown_ref, wsib_ref = refs[2 * count : 2 * count + 2]
    own_ref, sib_ref = refs[-2:]
    width = own_ref.shape[-1]
    z, s = place_of()
    for i in range(2):
        rows = pl.ds((1 - i) * width, width)
        for chunk, k in zip(refs[i * count : (i + 1) * count], ks):
            at = (z + s * k + 16) & (NZ - 1)
            value = chunk[...]
            own = contract_last(value, wown_ref[rows])
            sib = contract_last(value, wsib_ref[rows])
            for y in range(NY):
                for x in range(NX):
                    row = 8 * (y * NX + x)
                    own_ref[y, x, i, at] = own[row : row + 8]
                    sib_ref[FLIP[y], FLIP[x], i, at] = sib[row : row + 8].astype(bf16)


def outputs(acts, dpres, wown, wsib):
    width = wown.shape[0] // 2
    shapes = [((4, 4, 2, 8, 8, width), f32), ((4, 4, 2, 8, 8, width), bf16)]
    flops = 2 * 2 * 128 * wown.shape[1] * 2 * width
    most = (0, 1, 7, 2, 6, 3, 5)
    held = call(
        functools.partial(outputs_kernel, ks=most),
        shapes,
        *[chunks[k] for chunks in (acts, dpres) for k in most],
        wown,
        wsib,
        flops=7 * flops,
    )
    return call(
        functools.partial(outputs_kernel, ks=(4,)),
        shapes,
        acts[4],
        dpres[4],
        wown,
        wsib,
        *held,
        alias={4: 0, 5: 1},
        flops=flops,
    )


def grads_kernel(*refs):
    acts, dpres = refs[:NZ], refs[NZ : 2 * NZ]
    town_ref, tsib_ref, cown_ref, csib_ref, up_ref, down_ref, sib_ref = refs[2 * NZ : 2 * NZ + 7]
    act_ref, dpre_ref, own_ref, sems = refs[2 * NZ + 7 :]
    for k in range(NZ):
        act_ref[128 * k : 128 * k + 128] = acts[k][...]
        dpre_ref[128 * k : 128 * k + 128] = dpres[k][...]
    scale = 1.0 / math.sqrt(1024)
    hid = own_ref.shape[2]
    at = pl.multiple_of((lax.axis_index("row") & 1) * hid, 128)
    sib_ref[0] = contract_first(tsib_ref[...], dpre_ref[...]) * scale
    sib_ref[1] = contract_first(csib_ref[...], act_ref[...]) * scale
    copies = []
    for i, (left, right, out) in enumerate(
        ((town_ref, dpre_ref, up_ref), (cown_ref, act_ref, down_ref))
    ):
        own_ref[i] = contract_first(left[...], right[...]) * scale
        copies.append(
            pltpu.make_async_copy(own_ref.at[i], out.at[:, pl.ds(at, hid)], sems.at[i])
        )
        copies[-1].start()
    for copy in copies:
        copy.wait()


def place_kernel(sib_ref, up_in, down_in, up_ref, down_ref, sems):
    hid = sib_ref.shape[2]
    at = pl.multiple_of((1 - (lax.axis_index("row") & 1)) * hid, 128)
    copies = [
        pltpu.make_async_copy(sib_ref.at[i], out.at[:, pl.ds(at, hid)], sems.at[i])
        for i, out in enumerate((up_ref, down_ref))
    ]
    for copy in copies:
        copy.start()
    for copy in copies:
        copy.wait()


VMEM = pl.BlockSpec(memory_space=pltpu.VMEM)


def call(kernel, outs, *args, scratch=(), flops=0, alias=None, spaces=None, out_spaces=None):
    return pl.pallas_call(
        kernel,
        out_shape=[jax.ShapeDtypeStruct(shape, dtype) for shape, dtype in outs],
        in_specs=spaces or [VMEM] * len(args),
        out_specs=out_spaces or [VMEM] * len(outs),
        scratch_shapes=list(scratch),
        input_output_aliases=alias or {},
        compiler_params=pltpu.CompilerParams(vmem_limit_bytes=16 * 1024 * 1024),
        cost_estimate=pl.CostEstimate(flops=flops, bytes_accessed=4 << 20, transcendentals=0),
    )(*args)


ANY = pl.BlockSpec(memory_space=pl.ANY)


def gather_tokens(block):
    got = [swap("x", which, block) for which in (1, 2, 3)]
    both = [jnp.stack([block[i]] + [other[i] for other in got])[None] for i in range(2)]
    both = [jnp.concatenate([held, swap1("y", held)], axis=0) for held in both]
    both = [jnp.concatenate([held, swap2("y", held)], axis=0) for held in both]
    return got[0], both


def reduce_tokens(part):
    first = part[2:].astype(bf16)
    part = part[:2] + swap2("y", first).astype(f32)
    part = part[0] + swap1("y", part[1].astype(bf16)).astype(f32)
    return first, [part[0]] + [swap("x", which, part[which].astype(bf16)) for which in (1, 2, 3)]


def after(values, *earlier):
    held = lax.optimization_barrier((values, earlier))
    return held[0]


def reduce_z(parts):
    half = parts[0].shape[1] // 2
    sums, moving, last = [], [], ()
    for part in parts:
        sent = after((part[4][:half].astype(bf16), part[4][half:].astype(bf16)), *last)
        last = sent
        moving.append([swap1("z", sent[0]), swap2("z", sent[1])])
    for k in (3, 2, 1):
        for i, part in enumerate(parts):
            first, second = moving[i]
            second = after(second, *last).astype(f32)
            if k == 3:
                plus = jnp.concatenate([part[3][:half], part[3][half:] + second], axis=0)
            else:
                plus = part[k] + second
            plus = plus.astype(bf16)
            first = after(first, plus).astype(f32)
            if k == 3:
                minus = jnp.concatenate([part[5][:half] + first, part[5][half:]], axis=0)
            else:
                minus = part[8 - k] + first
            minus = minus.astype(bf16)
            last = (minus,)
            moving[i] = [swap1("z", plus), swap2("z", minus)]
    for i, part in enumerate(parts):
        first, second = after(tuple(moving[i]), *last)
        sums.append(part[0] + first.astype(f32) + second.astype(f32))
        last = (sums[-1],)
    return sums


def gather_z(owns):
    half = owns[0].shape[0] // 2
    gots = []
    for own in owns:
        gots.append({0: own, 1: swap1("z", own), 7: swap2("z", own)})
    for k in (2, 3):
        for got in gots:
            got[k] = swap1("z", got[9 - k])
            got[8 - k] = swap2("z", got[k - 1])
    sends = [(got[3][:half], got[5][half:]) for got in gots]
    for got, (front, back) in zip(gots, sends):
        got[4] = jnp.concatenate([swap2("z", front), swap1("z", back)], axis=0)
    return [[got[k] for k in range(8)] for got in gots], sends


def contract_last(left, right):
    return lax.dot_general(left, right, (((1,), (1,)), ((), ())), preferred_element_type=f32)


def contract_first(left, right):
    return lax.dot_general(left, right, (((0,), (0,)), ((), ())), preferred_element_type=f32)


def local(tokens, up_weight, down_weight, cotangent):
    core = lax.axis_index("row") % 2
    width = tokens.shape[1]
    hid = up_weight.shape[1] // 2

    block = jnp.stack([tokens.reshape(8, 8, width), cotangent.reshape(8, 8, width)])
    first, (tok16, cot16) = gather_tokens(block)

    up_weight, down_weight = after((up_weight, down_weight), first)
    weights = jnp.concatenate([up_weight, down_weight.T], axis=0)
    wown = lax.dynamic_slice_in_dim(weights, core * hid, hid, 1)
    wsib = core_swap(lax.dynamic_slice_in_dim(weights, (1 - core) * hid, hid, 1))

    def parts(mine, row):
        out = call(
            functools.partial(parts_kernel, row=row),
            [((8, 128, hid), f32), ((8, 128, width), bf16), ((8, 128, width), bf16)],
            mine,
            core_swap(mine),
            wown,
            wsib,
            flops=2 * 1024 * hid * 2 * width,
        )
        return out[0], out[1].reshape(1024, width), out[2].reshape(1024, width)

    pre_part, town, tsib = parts(tok16, 0)
    dact_part, cown, csib = parts(cot16, width)
    pre, dact = reduce_z([pre_part, dact_part])
    act, slope = gelu_and_slope(pre)
    (acts, dpres), sends = gather_z([act.astype(bf16), (dact * slope).astype(bf16)])

    own, sib = outputs(acts, dpres, *after((wown, wsib), *sends))
    first, terms = reduce_tokens(own + core_swap(sib).astype(f32))
    gu, gd, grad_sib = call(
        grads_kernel,
        [((width, 2 * hid), f32), ((width, 2 * hid), f32), ((2, width, hid), f32)],
        *acts,
        *dpres,
        *after((town, tsib, cown, csib), first),
        scratch=[
            pltpu.VMEM((1024, hid), bf16),
            pltpu.VMEM((1024, hid), bf16),
            pltpu.VMEM((2, width, hid), f32),
            pltpu.SemaphoreType.DMA((2,)),
        ],
        out_spaces=[ANY, ANY, VMEM],
        flops=2 * 2 * 1024 * hid * 2 * width,
    )
    gu, gd = call(
        place_kernel,
        [((width, 2 * hid), f32)] * 2,
        core_swap(grad_sib),
        gu,
        gd,
        scratch=[pltpu.SemaphoreType.DMA((2,))],
        alias={1: 0, 2: 1},
        spaces=[VMEM, ANY, ANY],
        out_spaces=[ANY, ANY],
    )
    terms[1:] = after(terms[1:], gu, gd)
    mixed, gtok = call(finish_kernel, [((8, 8, width), bf16)] * 2, *terms)
    return (mixed.reshape(64, width), gtok.reshape(64, width), gu, gd.T)


def solution(mesh):
    placed = (P("col", "row"), P("row", "col"), P("col", "row"), P("col", "row"))
    return jax.shard_map(
        local,
        mesh=mesh,
        in_specs=placed,
        out_specs=(P("col", "row"), P("col", "row"), P("row", "col"), P("col", "row")),
        check_vma=False,
    )
```

```python
import functools
import math

import jax
import jax.numpy as jnp
from jax import lax
from jax.experimental import pallas as pl
from jax.experimental.pallas import tpu as pltpu
from jax.sharding import PartitionSpec as P

root_coef = math.sqrt(2.0 / math.pi)
f32 = jnp.float32
bf16 = jnp.bfloat16

NZ = 8
NX = 4
NY = 4


def gelu_and_slope(value):
    inner = root_coef * (value + 0.044715 * value * value * value)
    tanh_val = jnp.tanh(inner)
    act = 0.5 * value * (1.0 + tanh_val)
    slope = 0.5 * (1.0 + tanh_val) + 0.5 * value * (1.0 - tanh_val * tanh_val) * root_coef * (
        1.0 + 3.0 * 0.044715 * value * value
    )
    return act, slope


def pairs(axis, which):
    out = []
    size = {"z": NZ, "x": NX, "y": NY}[axis]
    for z in range(NZ):
        for core in range(2):
            for x in range(NX):
                for y in range(NY):
                    at = {"z": z, "x": x, "y": y}
                    step = 1 if (at[axis] + core) % 2 == 0 else -1
                    at[axis] = (at[axis] + {1: step, 2: -step, 3: 2}[which]) % size
                    src = (z * 2 + core) * 16 + x * 4 + y
                    dst = (at["z"] * 2 + core) * 16 + at["x"] * 4 + at["y"]
                    out.append((src, dst))
    return out


PERMS = {
    (axis, which): pairs(axis, which) for axis in "xyz" for which in (1, 2, 3) if axis + str(which) != "z3"
}


def swap(axis, which, value):
    return lax.ppermute(value, ("row", "col"), PERMS[(axis, which)])


def swap1(axis, value):
    return swap(axis, 1, value)


def swap2(axis, value):
    return swap(axis, 2, value)


def core_swap(value):
    return lax.ppermute(value, "row", [(r, r ^ 1) for r in range(2 * NZ)])


def place_of():
    row = lax.axis_index("row")
    z = row // 2
    s = 1 - 2 * ((z + row) & 1)
    return z, s


FLIP = (0, 2, 1, 3)


def stack_kernel(own_ref, one_ref, two_ref, three_ref, tok_ref, cot_ref):
    for x, ref in enumerate((own_ref, one_ref, two_ref, three_ref)):
        tok_ref[x] = ref[0]
        cot_ref[x] = ref[1]


def finish_kernel(mix_own, gtok_own, one_ref, two_ref, three_ref, mix_ref, gtok_ref):
    for i, (own, out) in enumerate(((mix_own, mix_ref), (gtok_own, gtok_ref))):
        total = own[...]
        for ref in (one_ref, two_ref, three_ref):
            total += ref[i].astype(f32)
        out[...] = total.astype(out.dtype)


def token_chunk(owns, sibs, k):
    z, s = place_of()
    at = (z + s * k + 16) & (NZ - 1)
    own, sib = [], []
    for y in range(NY):
        for x in range(NX):
            own.append(owns[y // 2][y % 2, x, at].astype(f32))
            sib.append(sibs[FLIP[y] // 2][FLIP[y] % 2, FLIP[x], at].astype(f32))
    return jnp.concatenate(own, axis=0).astype(bf16), jnp.concatenate(sib, axis=0).astype(bf16)


def far_kernel(*refs, row):
    wown_ref, wsib_ref, plus_ref, minus_ref, town_ref, tsib_ref = refs[4:]
    rows = pl.ds(row, town_ref.shape[-1])
    own, sib = token_chunk(refs[:2], refs[2:4], 4)
    town_ref[4] = own
    tsib_ref[4] = sib
    part = jnp.dot(own, wown_ref[rows], preferred_element_type=f32) + jnp.dot(
        sib, wsib_ref[rows], preferred_element_type=f32
    )
    plus_ref[...] = part[:64].astype(bf16)
    minus_ref[...] = part[64:].astype(bf16)


def parts_kernel(*refs, row):
    wown_ref, wsib_ref, _, _, part_ref, town_ref, tsib_ref = refs[4:]
    rows = pl.ds(row, town_ref.shape[-1])
    for k in (3, 5, 2, 6, 1, 7, 0):
        own, sib = token_chunk(refs[:2], refs[2:4], k)
        town_ref[k] = own
        tsib_ref[k] = sib
        part_ref[k] = jnp.dot(own, wown_ref[rows], preferred_element_type=f32) + jnp.dot(
            sib, wsib_ref[rows], preferred_element_type=f32
        )


def outputs_kernel(*refs, ks):
    count = 2 * len(ks)
    wown_ref, wsib_ref = refs[count : count + 2]
    outs = refs[-4:]
    width = outs[0].shape[-1]
    z, s = place_of()
    for i in range(2):
        own_ref, sib_ref = outs[2 * i : 2 * i + 2]
        rows = pl.ds((1 - i) * width, width)
        for chunk, k in zip(refs[i * len(ks) : (i + 1) * len(ks)], ks):
            at = (z + s * k + 16) & (NZ - 1)
            value = chunk[...]
            own = contract_last(value, wown_ref[rows])
            sib = contract_last(value, wsib_ref[rows])
            for y in range(NY):
                for x in range(NX):
                    row = 8 * (y * NX + x)
                    own_ref[y, x, at] = own[row : row + 8]
                    sib_ref[FLIP[y], FLIP[x], at] = sib[row : row + 8].astype(bf16)


def outputs(acts, dpres, weights, sends):
    width = weights[0].shape[0] // 2
    shapes = [((4, 4, 8, 8, width), f32), ((4, 4, 8, 8, width), bf16)] * 2
    flops = 2 * 2 * 128 * weights[0].shape[1] * 2 * width
    most = (0, 1, 7, 2, 6, 3, 5)
    held = call(
        functools.partial(outputs_kernel, ks=most),
        shapes,
        *[chunks[k] for chunks in (acts, dpres) for k in most],
        *after(weights, *sends),
        flops=7 * flops,
    )
    held = call(
        functools.partial(outputs_kernel, ks=(4,)),
        shapes,
        acts[4],
        dpres[4],
        *weights,
        *held,
        alias={4 + i: i for i in range(4)},
        flops=flops,
    )
    return held[:2], held[2:]


def grads_kernel(*refs):
    acts, dpres = refs[:NZ], refs[NZ : 2 * NZ]
    town_ref, tsib_ref, cown_ref, csib_ref, up_ref, down_ref, sib_ref = refs[2 * NZ : 2 * NZ + 7]
    act_ref, dpre_ref, own_ref, sems = refs[2 * NZ + 7 :]
    for k in range(NZ):
        act_ref[128 * k : 128 * k + 128] = acts[k][...]
        dpre_ref[128 * k : 128 * k + 128] = dpres[k][...]
    scale = 1.0 / math.sqrt(1024)
    hid = own_ref.shape[2]
    at = pl.multiple_of((lax.axis_index("row") & 1) * hid, 128)
    sib_ref[0] = contract_first(tsib_ref[...], dpre_ref[...]) * scale
    sib_ref[1] = contract_first(csib_ref[...], act_ref[...]) * scale
    copies = []
    for i, (left, right, out) in enumerate(
        ((town_ref, dpre_ref, up_ref), (cown_ref, act_ref, down_ref))
    ):
        own_ref[i] = contract_first(left[...], right[...]) * scale
        copies.append(
            pltpu.make_async_copy(own_ref.at[i], out.at[:, pl.ds(at, hid)], sems.at[i])
        )
        copies[-1].start()
    for copy in copies:
        copy.wait()


def place_kernel(sib_ref, up_in, down_in, up_ref, down_ref, sems):
    hid = sib_ref.shape[2]
    at = pl.multiple_of((1 - (lax.axis_index("row") & 1)) * hid, 128)
    copies = [
        pltpu.make_async_copy(sib_ref.at[i], out.at[:, pl.ds(at, hid)], sems.at[i])
        for i, out in enumerate((up_ref, down_ref))
    ]
    for copy in copies:
        copy.start()
    for copy in copies:
        copy.wait()


VMEM = pl.BlockSpec(memory_space=pltpu.VMEM)


def call(kernel, outs, *args, scratch=(), flops=0, alias=None, spaces=None, out_spaces=None):
    return pl.pallas_call(
        kernel,
        out_shape=[jax.ShapeDtypeStruct(shape, dtype) for shape, dtype in outs],
        in_specs=spaces or [VMEM] * len(args),
        out_specs=out_spaces or [VMEM] * len(outs),
        scratch_shapes=list(scratch),
        input_output_aliases=alias or {},
        compiler_params=pltpu.CompilerParams(vmem_limit_bytes=16 * 1024 * 1024),
        cost_estimate=pl.CostEstimate(flops=flops, bytes_accessed=4 << 20, transcendentals=0),
    )(*args)


ANY = pl.BlockSpec(memory_space=pl.ANY)


def gather_tokens(block):
    got = [swap("x", which, block) for which in (1, 2, 3)]
    shape = (4,) + block.shape[1:]
    both = call(stack_kernel, [(shape, bf16)] * 2, block, *got)
    near = [jnp.stack([held, swap1("y", held)]) for held in both]
    far = [swap2("y", held) for held in near]
    near_sib = [core_swap(held) for held in near]
    return got[0], [(near[i], far[i], near_sib[i], core_swap(far[i])) for i in range(2)]


def reduce_tokens(pairs):
    last, moving, firsts = (), [], []
    for own, sib in pairs:
        part = own + after(core_swap(sib), *last).astype(f32)
        sent = part[2:].astype(bf16)
        last = (sent,)
        firsts.append(sent)
        moving.append((part[:2], swap2("y", sent)))
    for i, (keep, got) in enumerate(moving):
        part = keep + after(got, *last).astype(f32)
        sent = part[1].astype(bf16)
        last = (sent,)
        moving[i] = (part[0], swap1("y", sent))
    parts = [keep + after(got, *last).astype(f32) for keep, got in moving]
    lefts = [
        swap("x", which, jnp.stack([part[which] for part in parts]).astype(bf16)) for which in (1, 2, 3)
    ]
    return [part[0] for part in parts] + lefts, firsts


def after(values, *earlier):
    held = lax.optimization_barrier((values, earlier))
    return held[0]


def reduce_z(firsts, parts):
    half = parts[0].shape[1] // 2
    sums, last = [], ()
    moving = [[swap1("z", plus), swap2("z", minus)] for plus, minus in firsts]
    for k in (3, 2, 1):
        for i, part in enumerate(parts):
            first, second = moving[i]
            second = after(second, *last).astype(f32)
            if k == 3:
                plus = jnp.concatenate([part[3][:half], part[3][half:] + second], axis=0)
            else:
                plus = part[k] + second
            plus = plus.astype(bf16)
            first = after(first, plus).astype(f32)
            if k == 3:
                minus = jnp.concatenate([part[5][:half] + first, part[5][half:]], axis=0)
            else:
                minus = part[8 - k] + first
            minus = minus.astype(bf16)
            last = (minus,)
            moving[i] = [swap1("z", plus), swap2("z", minus)]
    for i, part in enumerate(parts):
        first, second = after(tuple(moving[i]), *last)
        sums.append(part[0] + first.astype(f32) + second.astype(f32))
        last = (sums[-1],)
    return sums


def gather_z(owns):
    half = owns[0].shape[0] // 2
    gots = [{0: own, 1: swap1("z", own), 7: swap2("z", own)} for own in owns]
    for k in (2, 3):
        last = ()
        for got in gots:
            got[k - 1], got[9 - k] = after((got[k - 1], got[9 - k]), *last)
            last = (got[k - 1], got[9 - k])
            got[k] = swap1("z", got[9 - k])
            got[8 - k] = swap2("z", got[k - 1])
    last, sends = (), []
    for got in gots:
        got[3], got[5] = after((got[3], got[5]), *last)
        last = (got[3][:half], got[5][half:])
        sends.append(last)
        got[4] = jnp.concatenate([swap2("z", last[0]), swap1("z", last[1])], axis=0)
    return [[got[k] for k in range(8)] for got in gots], sends


def contract_last(left, right):
    return lax.dot_general(left, right, (((1,), (1,)), ((), ())), preferred_element_type=f32)


def contract_first(left, right):
    return lax.dot_general(left, right, (((0,), (0,)), ((), ())), preferred_element_type=f32)


def local(tokens, up_weight, down_weight, cotangent):
    core = lax.axis_index("row") % 2
    width = tokens.shape[1]
    hid = up_weight.shape[1] // 2

    block = jnp.stack([tokens.reshape(8, 8, width), cotangent.reshape(8, 8, width)])
    first, (tok_parts, cot_parts) = gather_tokens(block)

    up_weight, down_weight = after((up_weight, down_weight), first)
    weights = jnp.concatenate([up_weight, down_weight.T], axis=0)
    wown = lax.dynamic_slice_in_dim(weights, core * hid, hid, 1)
    wsib = core_swap(lax.dynamic_slice_in_dim(weights, (1 - core) * hid, hid, 1))

    def far(pieces, row):
        return call(
            functools.partial(far_kernel, row=row),
            [((64, hid), bf16)] * 2 + [((8, 128, width), bf16)] * 2,
            *pieces,
            wown,
            wsib,
            flops=2 * 128 * hid * 2 * width,
        )

    def parts(pieces, row, town, tsib):
        out = call(
            functools.partial(parts_kernel, row=row),
            [((8, 128, hid), f32), ((8, 128, width), bf16), ((8, 128, width), bf16)],
            *pieces,
            *after((wown, wsib), *sends),
            town,
            tsib,
            alias={6: 1, 7: 2},
            flops=2 * 1024 * hid * 2 * width,
        )
        return out[0], out[1].reshape(1024, width), out[2].reshape(1024, width)

    *tok_far, town, tsib = far(tok_parts, 0)
    *cot_far, cown, csib = far(cot_parts, width)
    sends = tok_far + cot_far
    pre_part, town, tsib = parts(tok_parts, 0, town, tsib)
    dact_part, cown, csib = parts(cot_parts, width, cown, csib)
    pre, dact = reduce_z([tok_far, cot_far], [pre_part, dact_part])
    act, slope = gelu_and_slope(pre)
    (acts, dpres), sends = gather_z([act.astype(bf16), (dact * slope).astype(bf16)])

    pairs = outputs(acts, dpres, (wown, wsib), sends)
    lefts, firsts = reduce_tokens(pairs)
    gu, gd, grad_sib = call(
        grads_kernel,
        [((width, 2 * hid), f32), ((width, 2 * hid), f32), ((2, width, hid), f32)],
        *acts,
        *dpres,
        *after((town, tsib, cown, csib), *firsts),
        scratch=[
            pltpu.VMEM((1024, hid), bf16),
            pltpu.VMEM((1024, hid), bf16),
            pltpu.VMEM((2, width, hid), f32),
            pltpu.SemaphoreType.DMA((2,)),
        ],
        out_spaces=[ANY, ANY, VMEM],
        flops=2 * 2 * 1024 * hid * 2 * width,
    )
    gu, gd = call(
        place_kernel,
        [((width, 2 * hid), f32)] * 2,
        core_swap(grad_sib),
        gu,
        gd,
        scratch=[pltpu.SemaphoreType.DMA((2,))],
        alias={1: 0, 2: 1},
        spaces=[VMEM, ANY, ANY],
        out_spaces=[ANY, ANY],
    )
    lefts[2:] = after(lefts[2:], gu, gd)
    mixed, gtok = call(finish_kernel, [((8, 8, width), bf16)] * 2, *lefts)
    return (mixed.reshape(64, width), gtok.reshape(64, width), gu, gd.T)


def solution(mesh):
    placed = (P("col", "row"), P("row", "col"), P("col", "row"), P("col", "row"))
    return jax.shard_map(
        local,
        mesh=mesh,
        in_specs=placed,
        out_specs=(P("col", "row"), P("col", "row"), P("row", "col"), P("col", "row")),
        check_vma=False,
    )
```

```python
import functools
import math

import jax
import jax.numpy as jnp
from jax import lax
from jax.experimental import pallas as pl
from jax.experimental.pallas import tpu as pltpu
from jax.sharding import PartitionSpec as P

root_coef = math.sqrt(2.0 / math.pi)
f32 = jnp.float32
bf16 = jnp.bfloat16

NZ = 8
NX = 4
NY = 4


def gelu_and_slope(value):
    inner = root_coef * (value + 0.044715 * value * value * value)
    tanh_val = jnp.tanh(inner)
    act = 0.5 * value * (1.0 + tanh_val)
    slope = 0.5 * (1.0 + tanh_val) + 0.5 * value * (1.0 - tanh_val * tanh_val) * root_coef * (
        1.0 + 3.0 * 0.044715 * value * value
    )
    return act, slope


def pairs(axis, which):
    out = []
    size = {"z": NZ, "x": NX, "y": NY}[axis]
    for z in range(NZ):
        for core in range(2):
            for x in range(NX):
                for y in range(NY):
                    at = {"z": z, "x": x, "y": y}
                    step = 1 if (at[axis] + core) % 2 == 0 else -1
                    at[axis] = (at[axis] + {1: step, 2: -step, 3: 2}[which]) % size
                    src = (z * 2 + core) * 16 + x * 4 + y
                    dst = (at["z"] * 2 + core) * 16 + at["x"] * 4 + at["y"]
                    out.append((src, dst))
    return out


PERMS = {
    (axis, which): pairs(axis, which) for axis in "xyz" for which in (1, 2, 3) if axis + str(which) != "z3"
}


def swap(axis, which, value):
    return lax.ppermute(value, ("row", "col"), PERMS[(axis, which)])


def swap1(axis, value):
    return swap(axis, 1, value)


def swap2(axis, value):
    return swap(axis, 2, value)


def core_swap(value):
    return lax.ppermute(value, "row", [(r, r ^ 1) for r in range(2 * NZ)])


def place_of():
    row = lax.axis_index("row")
    z = row // 2
    s = 1 - 2 * ((z + row) & 1)
    return z, s


FLIP = (0, 2, 1, 3)


def stack_kernel(own_ref, one_ref, two_ref, three_ref, tok_ref, cot_ref):
    for x, ref in enumerate((own_ref, one_ref, two_ref, three_ref)):
        tok_ref[x] = ref[0]
        cot_ref[x] = ref[1]


def finish_kernel(mix_own, gtok_own, one_ref, two_ref, three_ref, mix_ref, gtok_ref):
    for i, (own, out) in enumerate(((mix_own, mix_ref), (gtok_own, gtok_ref))):
        total = own[...]
        for ref in (one_ref, two_ref, three_ref):
            total += ref[i].astype(f32)
        out[...] = total.astype(out.dtype)


def token_chunk(owns, sibs, k):
    z, s = place_of()
    at = (z + s * k + 16) & (NZ - 1)
    own, sib = [], []
    for y in range(NY):
        for x in range(NX):
            own.append(owns[y // 2][y % 2, x, at].astype(f32))
            sib.append(sibs[FLIP[y] // 2][FLIP[y] % 2, FLIP[x], at].astype(f32))
    return jnp.concatenate(own, axis=0).astype(bf16), jnp.concatenate(sib, axis=0).astype(bf16)


def far_kernel(*refs, row):
    wown_ref, wsib_ref, part_ref, town_ref, tsib_ref = refs[4:]
    rows = pl.ds(row, town_ref.shape[-1])
    own, sib = token_chunk(refs[:2], refs[2:4], 4)
    town_ref[4] = own
    tsib_ref[4] = sib
    part = jnp.dot(own, wown_ref[rows], preferred_element_type=f32) + jnp.dot(
        sib, wsib_ref[rows], preferred_element_type=f32
    )
    part_ref[...] = part.astype(bf16)


def parts_kernel(*refs, row):
    wown_ref, wsib_ref, _, _, part_ref, town_ref, tsib_ref = refs[4:]
    rows = pl.ds(row, town_ref.shape[-1])
    for k in (3, 5, 2, 6, 1, 7, 0):
        own, sib = token_chunk(refs[:2], refs[2:4], k)
        town_ref[k] = own
        tsib_ref[k] = sib
        part_ref[k] = jnp.dot(own, wown_ref[rows], preferred_element_type=f32) + jnp.dot(
            sib, wsib_ref[rows], preferred_element_type=f32
        )


def outputs_kernel(*refs, ks):
    count = 2 * len(ks)
    wown_ref, wsib_ref = refs[count : count + 2]
    outs = refs[-4:]
    width = outs[0].shape[-1]
    z, s = place_of()
    for i in range(2):
        own_ref, sib_ref = outs[2 * i : 2 * i + 2]
        rows = pl.ds((1 - i) * width, width)
        for chunk, k in zip(refs[i * len(ks) : (i + 1) * len(ks)], ks):
            at = (z + s * k + 16) & (NZ - 1)
            value = chunk[...]
            own = contract_last(value, wown_ref[rows])
            sib = contract_last(value, wsib_ref[rows])
            for y in range(NY):
                for x in range(NX):
                    row = 8 * (y * NX + x)
                    own_ref[y, x, at] = own[row : row + 8]
                    sib_ref[FLIP[y], FLIP[x], at] = sib[row : row + 8].astype(bf16)


def outputs(acts, dpres, weights):
    width = weights[0].shape[0] // 2
    shapes = [((4, 4, 8, 8, width), f32), ((4, 4, 8, 8, width), bf16)] * 2
    flops = 2 * 2 * 128 * weights[0].shape[1] * 2 * width
    most = (0, 1, 7, 2, 6, 3, 5)
    held = call(
        functools.partial(outputs_kernel, ks=most),
        shapes,
        *[chunks[k] for chunks in (acts, dpres) for k in most],
        *weights,
        flops=7 * flops,
    )
    held = call(
        functools.partial(outputs_kernel, ks=(4,)),
        shapes,
        acts[4],
        dpres[4],
        *weights,
        *held,
        alias={4 + i: i for i in range(4)},
        flops=flops,
    )
    return held[:2], held[2:]


def grads_kernel(*refs):
    acts, dpres = refs[:NZ], refs[NZ : 2 * NZ]
    town_ref, tsib_ref, cown_ref, csib_ref, up_ref, down_ref, sib_ref = refs[2 * NZ : 2 * NZ + 7]
    act_ref, dpre_ref, own_ref, sems = refs[2 * NZ + 7 :]
    for k in range(NZ):
        act_ref[128 * k : 128 * k + 128] = acts[k][...]
        dpre_ref[128 * k : 128 * k + 128] = dpres[k][...]
    scale = 1.0 / math.sqrt(1024)
    hid = own_ref.shape[2]
    at = pl.multiple_of((lax.axis_index("row") & 1) * hid, 128)
    sib_ref[0] = contract_first(tsib_ref[...], dpre_ref[...]) * scale
    sib_ref[1] = contract_first(csib_ref[...], act_ref[...]) * scale
    copies = []
    for i, (left, right, out) in enumerate(
        ((town_ref, dpre_ref, up_ref), (cown_ref, act_ref, down_ref))
    ):
        own_ref[i] = contract_first(left[...], right[...]) * scale
        copies.append(
            pltpu.make_async_copy(own_ref.at[i], out.at[:, pl.ds(at, hid)], sems.at[i])
        )
        copies[-1].start()
    for copy in copies:
        copy.wait()


def place_kernel(sib_ref, up_in, down_in, up_ref, down_ref, sems):
    hid = sib_ref.shape[2]
    at = pl.multiple_of((1 - (lax.axis_index("row") & 1)) * hid, 128)
    copies = [
        pltpu.make_async_copy(sib_ref.at[i], out.at[:, pl.ds(at, hid)], sems.at[i])
        for i, out in enumerate((up_ref, down_ref))
    ]
    for copy in copies:
        copy.start()
    for copy in copies:
        copy.wait()


VMEM = pl.BlockSpec(memory_space=pltpu.VMEM)


def call(kernel, outs, *args, scratch=(), flops=0, alias=None, spaces=None, out_spaces=None):
    return pl.pallas_call(
        kernel,
        out_shape=[jax.ShapeDtypeStruct(shape, dtype) for shape, dtype in outs],
        in_specs=spaces or [VMEM] * len(args),
        out_specs=out_spaces or [VMEM] * len(outs),
        scratch_shapes=list(scratch),
        input_output_aliases=alias or {},
        compiler_params=pltpu.CompilerParams(vmem_limit_bytes=16 * 1024 * 1024),
        cost_estimate=pl.CostEstimate(flops=flops, bytes_accessed=4 << 20, transcendentals=0),
    )(*args)


ANY = pl.BlockSpec(memory_space=pl.ANY)


def gather_tokens(block):
    got = [swap("x", which, block) for which in (1, 2, 3)]
    shape = (4,) + block.shape[1:]
    both = call(stack_kernel, [(shape, bf16)] * 2, block, *got)
    near = [jnp.stack([held, swap1("y", held)]) for held in both]
    far = [swap2("y", held) for held in near]
    near_sib = [core_swap(held) for held in near]
    return got[0], [(near[i], far[i], near_sib[i], core_swap(far[i])) for i in range(2)]


def reduce_tokens(pairs):
    last, moving, firsts = (), [], []
    for own, sib in pairs:
        part = own + after(core_swap(sib), *last).astype(f32)
        sent = part[2:].astype(bf16)
        last = (sent,)
        firsts.append(sent)
        moving.append((part[:2], swap2("y", sent)))
    for i, (keep, got) in enumerate(moving):
        part = keep + after(got, *last).astype(f32)
        sent = part[1].astype(bf16)
        last = (sent,)
        moving[i] = (part[0], swap1("y", sent))
    parts = [keep + after(got, *last).astype(f32) for keep, got in moving]
    lefts = [
        swap("x", which, jnp.stack([part[which] for part in parts]).astype(bf16)) for which in (1, 2, 3)
    ]
    return [part[0] for part in parts] + lefts, firsts


def after(values, *earlier):
    held = lax.optimization_barrier((values, earlier))
    return held[0]


TURNS = (((0, 1), (1, 2), (0, 2), (1, 1)), ((0, 2), (1, 1), (0, 1), (1, 2)))


def reduce_z(firsts, parts):
    last = ()
    got = {(0, 1): swap1("z", firsts[0]), (1, 2): swap2("z", firsts[1])}
    for k in (3, 2, 1):
        sent = {}
        for i, way in TURNS[(3 - k) % 2]:
            part = parts[i][k if way == 1 else 8 - k]
            if (i, 3 - way) in got:
                part = part + after(got[(i, 3 - way)], *last).astype(f32)
            part = part.astype(bf16)
            last = (part,)
            sent[(i, way)] = swap("z", way, part)
        got = sent
    sums = []
    for i, part in enumerate(parts):
        first, second = after((got[(i, 1)], got[(i, 2)]), *last)
        sums.append(part[0] + first.astype(f32) + second.astype(f32))
        last = (sums[-1],)
    return sums


def gather_z(owns):
    gots = [{0: own} for own in owns]
    for i, way in TURNS[0]:
        gots[i][1 if way == 1 else 7] = swap("z", way, owns[i])
    last = ()
    for k in (2, 3, 4):
        for i, way in TURNS[(k - 1) % 2]:
            got = gots[i]
            at = 9 - k if way == 1 else k - 1
            got[at] = after(got[at], *last)
            last = (got[at],)
            if k < 4:
                got[k if way == 1 else 8 - k] = swap("z", way, got[at])
            elif way == 2 - i:
                got[4] = swap("z", way, got[at])
    return [[got[k] for k in range(8)] for got in gots]


def contract_last(left, right):
    return lax.dot_general(left, right, (((1,), (1,)), ((), ())), preferred_element_type=f32)


def contract_first(left, right):
    return lax.dot_general(left, right, (((0,), (0,)), ((), ())), preferred_element_type=f32)


def local(tokens, up_weight, down_weight, cotangent):
    core = lax.axis_index("row") % 2
    width = tokens.shape[1]
    hid = up_weight.shape[1] // 2

    block = jnp.stack([tokens.reshape(8, 8, width), cotangent.reshape(8, 8, width)])
    first, (tok_parts, cot_parts) = gather_tokens(block)

    up_weight, down_weight = after((up_weight, down_weight), first)
    weights = jnp.concatenate([up_weight, down_weight.T], axis=0)
    wown = lax.dynamic_slice_in_dim(weights, core * hid, hid, 1)
    wsib = core_swap(lax.dynamic_slice_in_dim(weights, (1 - core) * hid, hid, 1))

    def far(pieces, row):
        return call(
            functools.partial(far_kernel, row=row),
            [((128, hid), bf16)] + [((8, 128, width), bf16)] * 2,
            *pieces,
            wown,
            wsib,
            flops=2 * 128 * hid * 2 * width,
        )

    def parts(pieces, row, town, tsib):
        out = call(
            functools.partial(parts_kernel, row=row),
            [((8, 128, hid), f32), ((8, 128, width), bf16), ((8, 128, width), bf16)],
            *pieces,
            *after((wown, wsib), *sends),
            town,
            tsib,
            alias={6: 1, 7: 2},
            flops=2 * 1024 * hid * 2 * width,
        )
        return out[0], out[1].reshape(1024, width), out[2].reshape(1024, width)

    tok_far, town, tsib = far(tok_parts, 0)
    cot_far, cown, csib = far(cot_parts, width)
    sends = (tok_far, cot_far)
    pre_part, town, tsib = parts(tok_parts, 0, town, tsib)
    dact_part, cown, csib = parts(cot_parts, width, cown, csib)
    pre, dact = reduce_z([tok_far, cot_far], [pre_part, dact_part])
    act, slope = gelu_and_slope(pre)
    acts, dpres = gather_z([act.astype(bf16), (dact * slope).astype(bf16)])

    pairs = outputs(acts, dpres, (wown, wsib))
    lefts, firsts = reduce_tokens(pairs)
    gu, gd, grad_sib = call(
        grads_kernel,
        [((width, 2 * hid), f32), ((width, 2 * hid), f32), ((2, width, hid), f32)],
        *acts,
        *dpres,
        *after((town, tsib, cown, csib), *firsts),
        scratch=[
            pltpu.VMEM((1024, hid), bf16),
            pltpu.VMEM((1024, hid), bf16),
            pltpu.VMEM((2, width, hid), f32),
            pltpu.SemaphoreType.DMA((2,)),
        ],
        out_spaces=[ANY, ANY, VMEM],
        flops=2 * 2 * 1024 * hid * 2 * width,
    )
    gu, gd = call(
        place_kernel,
        [((width, 2 * hid), f32)] * 2,
        core_swap(grad_sib),
        gu,
        gd,
        scratch=[pltpu.SemaphoreType.DMA((2,))],
        alias={1: 0, 2: 1},
        spaces=[VMEM, ANY, ANY],
        out_spaces=[ANY, ANY],
    )
    lefts[2:] = after(lefts[2:], gu, gd)
    mixed, gtok = call(finish_kernel, [((8, 8, width), bf16)] * 2, *lefts)
    return (mixed.reshape(64, width), gtok.reshape(64, width), gu, gd.T)


def solution(mesh):
    placed = (P("col", "row"), P("row", "col"), P("col", "row"), P("col", "row"))
    return jax.shard_map(
        local,
        mesh=mesh,
        in_specs=placed,
        out_specs=(P("col", "row"), P("col", "row"), P("row", "col"), P("col", "row")),
        check_vma=False,
    )
```

```python
import functools
import math

import jax
import jax.numpy as jnp
from jax import lax
from jax.experimental import pallas as pl
from jax.experimental.pallas import tpu as pltpu
from jax.sharding import PartitionSpec as P

root_coef = math.sqrt(2.0 / math.pi)
f32 = jnp.float32
bf16 = jnp.bfloat16

NZ = 8
NX = 4
NY = 4


def gelu_and_slope(value):
    inner = root_coef * (value + 0.044715 * value * value * value)
    tanh_val = jnp.tanh(inner)
    act = 0.5 * value * (1.0 + tanh_val)
    slope = 0.5 * (1.0 + tanh_val) + 0.5 * value * (1.0 - tanh_val * tanh_val) * root_coef * (
        1.0 + 3.0 * 0.044715 * value * value
    )
    return act, slope


def pairs(axis, which):
    out = []
    size = {"z": NZ, "x": NX, "y": NY}[axis]
    for z in range(NZ):
        for core in range(2):
            for x in range(NX):
                for y in range(NY):
                    at = {"z": z, "x": x, "y": y}
                    step = 1 if (at[axis] + core) % 2 == 0 else -1
                    at[axis] = (at[axis] + {1: step, 2: -step, 3: 2}[which]) % size
                    src = (z * 2 + core) * 16 + x * 4 + y
                    dst = (at["z"] * 2 + core) * 16 + at["x"] * 4 + at["y"]
                    out.append((src, dst))
    return out


PERMS = {
    (axis, which): pairs(axis, which) for axis in "xyz" for which in (1, 2, 3) if axis + str(which) != "z3"
}


def swap(axis, which, value):
    return lax.ppermute(value, ("row", "col"), PERMS[(axis, which)])


def swap1(axis, value):
    return swap(axis, 1, value)


def swap2(axis, value):
    return swap(axis, 2, value)


def core_swap(value):
    return lax.ppermute(value, "row", [(r, r ^ 1) for r in range(2 * NZ)])


def place_of():
    row = lax.axis_index("row")
    z = row // 2
    s = 1 - 2 * ((z + row) & 1)
    return z, s


FLIP = (0, 2, 1, 3)


def stack_kernel(own_ref, one_ref, two_ref, three_ref, tok_ref, cot_ref):
    for x, ref in enumerate((own_ref, one_ref, two_ref, three_ref)):
        tok_ref[x] = ref[0]
        cot_ref[x] = ref[1]


def finish_kernel(mix_own, gtok_own, one_ref, two_ref, three_ref, mix_ref, gtok_ref):
    for i, (own, out) in enumerate(((mix_own, mix_ref), (gtok_own, gtok_ref))):
        total = own[...]
        for ref in (one_ref, two_ref, three_ref):
            total += ref[i].astype(f32)
        out[...] = total.astype(out.dtype)


def token_chunk(owns, sibs, k):
    z, s = place_of()
    at = (z + s * k + 16) & (NZ - 1)
    own, sib = [], []
    for y in range(NY):
        for x in range(NX):
            own.append(owns[y // 2][y % 2, x, at].astype(f32))
            sib.append(sibs[FLIP[y] // 2][FLIP[y] % 2, FLIP[x], at].astype(f32))
    return jnp.concatenate(own, axis=0).astype(bf16), jnp.concatenate(sib, axis=0).astype(bf16)


def far_kernel(*refs, row):
    wown_ref, wsib_ref, part_ref, town_ref, tsib_ref = refs[4:]
    rows = pl.ds(row, town_ref.shape[-1])
    own, sib = token_chunk(refs[:2], refs[2:4], 4)
    town_ref[4] = own
    tsib_ref[4] = sib
    part = jnp.dot(own, wown_ref[rows], preferred_element_type=f32) + jnp.dot(
        sib, wsib_ref[rows], preferred_element_type=f32
    )
    part_ref[...] = part.astype(bf16)


def parts_kernel(*refs, row):
    wown_ref, wsib_ref, _, _, part_ref, town_ref, tsib_ref = refs[4:]
    rows = pl.ds(row, town_ref.shape[-1])
    for k in (3, 5, 2, 6, 1, 7, 0):
        own, sib = token_chunk(refs[:2], refs[2:4], k)
        town_ref[k] = own
        tsib_ref[k] = sib
        part_ref[k] = jnp.dot(own, wown_ref[rows], preferred_element_type=f32) + jnp.dot(
            sib, wsib_ref[rows], preferred_element_type=f32
        )


def outputs_kernel(*refs, ks):
    count = 2 * len(ks)
    wown_ref, wsib_ref = refs[count : count + 2]
    outs = refs[-4:]
    width = outs[0].shape[-1]
    z, s = place_of()
    for i in range(2):
        own_ref, sib_ref = outs[2 * i : 2 * i + 2]
        rows = pl.ds((1 - i) * width, width)
        for chunk, k in zip(refs[i * len(ks) : (i + 1) * len(ks)], ks):
            at = (z + s * k + 16) & (NZ - 1)
            value = chunk[...]
            own = contract_last(value, wown_ref[rows])
            sib = contract_last(value, wsib_ref[rows])
            for y in range(NY):
                for x in range(NX):
                    row = 8 * (y * NX + x)
                    own_ref[y, x, at] = own[row : row + 8]
                    sib_ref[FLIP[y], FLIP[x], at] = sib[row : row + 8].astype(bf16)


def outputs(acts, dpres, weights):
    width = weights[0].shape[0] // 2
    shapes = [((4, 4, 8, 8, width), f32), ((4, 4, 8, 8, width), bf16)] * 2
    flops = 2 * 2 * 128 * weights[0].shape[1] * 2 * width
    most = (0, 1, 7, 2, 6, 3, 5)
    held = call(
        functools.partial(outputs_kernel, ks=most),
        shapes,
        *[chunks[k] for chunks in (acts, dpres) for k in most],
        *weights,
        flops=7 * flops,
    )
    held = call(
        functools.partial(outputs_kernel, ks=(4,)),
        shapes,
        acts[4],
        dpres[4],
        *weights,
        *held,
        alias={4 + i: i for i in range(4)},
        flops=flops,
    )
    return held[:2], held[2:]


def grads_kernel(*refs):
    acts, dpres = refs[:NZ], refs[NZ : 2 * NZ]
    town_ref, tsib_ref, cown_ref, csib_ref, up_ref, down_ref, sib_ref = refs[2 * NZ : 2 * NZ + 7]
    act_ref, dpre_ref, own_ref, sems = refs[2 * NZ + 7 :]
    for k in range(NZ):
        act_ref[128 * k : 128 * k + 128] = acts[k][...]
        dpre_ref[128 * k : 128 * k + 128] = dpres[k][...]
    scale = 1.0 / math.sqrt(1024)
    hid = own_ref.shape[2]
    at = pl.multiple_of((lax.axis_index("row") & 1) * hid, 128)
    sib_ref[0] = contract_first(tsib_ref[...], dpre_ref[...]) * scale
    sib_ref[1] = contract_first(csib_ref[...], act_ref[...]) * scale
    copies = []
    for i, (left, right, out) in enumerate(
        ((town_ref, dpre_ref, up_ref), (cown_ref, act_ref, down_ref))
    ):
        own_ref[i] = contract_first(left[...], right[...]) * scale
        copies.append(
            pltpu.make_async_copy(own_ref.at[i], out.at[:, pl.ds(at, hid)], sems.at[i])
        )
        copies[-1].start()
    for copy in copies:
        copy.wait()


def place_kernel(sib_ref, up_in, down_in, up_ref, down_ref, sems):
    hid = sib_ref.shape[2]
    at = pl.multiple_of((1 - (lax.axis_index("row") & 1)) * hid, 128)
    copies = [
        pltpu.make_async_copy(sib_ref.at[i], out.at[:, pl.ds(at, hid)], sems.at[i])
        for i, out in enumerate((up_ref, down_ref))
    ]
    for copy in copies:
        copy.start()
    for copy in copies:
        copy.wait()


VMEM = pl.BlockSpec(memory_space=pltpu.VMEM)


def call(kernel, outs, *args, scratch=(), flops=0, alias=None, spaces=None, out_spaces=None):
    return pl.pallas_call(
        kernel,
        out_shape=[jax.ShapeDtypeStruct(shape, dtype) for shape, dtype in outs],
        in_specs=spaces or [VMEM] * len(args),
        out_specs=out_spaces or [VMEM] * len(outs),
        scratch_shapes=list(scratch),
        input_output_aliases=alias or {},
        compiler_params=pltpu.CompilerParams(vmem_limit_bytes=16 * 1024 * 1024),
        cost_estimate=pl.CostEstimate(flops=flops, bytes_accessed=4 << 20, transcendentals=0),
    )(*args)


ANY = pl.BlockSpec(memory_space=pl.ANY)


def gather_tokens(block):
    got = [swap("x", which, block) for which in (1, 2, 3)]
    shape = (4,) + block.shape[1:]
    both = call(stack_kernel, [(shape, bf16)] * 2, block, *got)
    near = [jnp.stack([held, swap1("y", held)]) for held in both]
    far = [swap2("y", held) for held in near]
    near_sib = [core_swap(held) for held in near]
    return got[0], [(near[i], far[i], near_sib[i], core_swap(far[i])) for i in range(2)]


def reduce_tokens(pairs):
    last, moving, firsts = (), [], []
    for own, sib in pairs:
        part = own + after(core_swap(sib), *last).astype(f32)
        sent = part[2:].astype(bf16)
        last = (sent,)
        firsts.append(sent)
        moving.append((part[:2], swap2("y", sent)))
    for i, (keep, got) in enumerate(moving):
        part = keep + after(got, *last).astype(f32)
        sent = part[1].astype(bf16)
        last = (sent,)
        moving[i] = (part[0], swap1("y", sent))
    parts = [keep + after(got, *last).astype(f32) for keep, got in moving]
    sent, last = [], ()
    for which in (3, 2, 1):
        pair = after([part[which] for part in parts], *last)
        sent.append(jnp.stack(pair).astype(bf16))
        last = (sent[-1],)
    lefts = [swap("x", 3 - i, value) for i, value in enumerate(sent)]
    return [part[0] for part in parts] + lefts, firsts


def after(values, *earlier):
    held = lax.optimization_barrier((values, earlier))
    return held[0]


TURNS = (((0, 1), (1, 2), (0, 2), (1, 1)), ((0, 2), (1, 1), (0, 1), (1, 2)))


def reduce_z(firsts, parts):
    last = ()
    got = {(0, 1): swap1("z", firsts[0]), (1, 2): swap2("z", firsts[1])}
    for k in (3, 2, 1):
        sent = {}
        for i, way in (TURNS[(3 - k) % 2] if k > 1 else ((0, 1), (0, 2), (1, 2), (1, 1))):
            part = parts[i][k if way == 1 else 8 - k]
            if (i, 3 - way) in got:
                part = part + after(got[(i, 3 - way)], *last).astype(f32)
            part = part.astype(bf16)
            last = (part,)
            sent[(i, way)] = swap("z", way, part)
        got = sent
    sums = []
    for i, part in enumerate(parts):
        first, second = after((got[(i, 1)], got[(i, 2)]), *last)
        sums.append(part[0] + first.astype(f32) + second.astype(f32))
        last = (sums[-1],)
    return sums


def gather_z(owns):
    gots = [{0: own} for own in owns]
    for i, way in TURNS[0]:
        gots[i][1 if way == 1 else 7] = swap("z", way, owns[i])
    last = ()
    for k in (2, 3, 4):
        for i, way in TURNS[(k - 1) % 2]:
            got = gots[i]
            at = 9 - k if way == 1 else k - 1
            got[at] = after(got[at], *last)
            last = (got[at],)
            if k < 4:
                got[k if way == 1 else 8 - k] = swap("z", way, got[at])
            elif way == 2 - i:
                got[4] = swap("z", way, got[at])
    return [[got[k] for k in range(8)] for got in gots]


def contract_last(left, right):
    return lax.dot_general(left, right, (((1,), (1,)), ((), ())), preferred_element_type=f32)


def contract_first(left, right):
    return lax.dot_general(left, right, (((0,), (0,)), ((), ())), preferred_element_type=f32)


def local(tokens, up_weight, down_weight, cotangent):
    core = lax.axis_index("row") % 2
    width = tokens.shape[1]
    hid = up_weight.shape[1] // 2

    block = jnp.stack([tokens.reshape(8, 8, width), cotangent.reshape(8, 8, width)])
    first, (tok_parts, cot_parts) = gather_tokens(block)

    up_weight, down_weight = after((up_weight, down_weight), first)
    weights = jnp.concatenate([up_weight, down_weight.T], axis=0)
    wown = lax.dynamic_slice_in_dim(weights, core * hid, hid, 1)
    wsib = core_swap(lax.dynamic_slice_in_dim(weights, (1 - core) * hid, hid, 1))

    def far(pieces, row):
        return call(
            functools.partial(far_kernel, row=row),
            [((128, hid), bf16)] + [((8, 128, width), bf16)] * 2,
            *pieces,
            wown,
            wsib,
            flops=2 * 128 * hid * 2 * width,
        )

    def parts(pieces, row, town, tsib):
        out = call(
            functools.partial(parts_kernel, row=row),
            [((8, 128, hid), f32), ((8, 128, width), bf16), ((8, 128, width), bf16)],
            *pieces,
            *after((wown, wsib), *sends),
            town,
            tsib,
            alias={6: 1, 7: 2},
            flops=2 * 1024 * hid * 2 * width,
        )
        return out[0], out[1].reshape(1024, width), out[2].reshape(1024, width)

    tok_far, town, tsib = far(tok_parts, 0)
    cot_far, cown, csib = far(cot_parts, width)
    sends = (tok_far, cot_far)
    pre_part, town, tsib = parts(tok_parts, 0, town, tsib)
    dact_part, cown, csib = parts(cot_parts, width, cown, csib)
    pre, dact = reduce_z([tok_far, cot_far], [pre_part, dact_part])
    act, slope = gelu_and_slope(pre)
    acts, dpres = gather_z([act.astype(bf16), (dact * slope).astype(bf16)])

    pairs = outputs(acts, dpres, (wown, wsib))
    lefts, firsts = reduce_tokens(pairs)
    gu, gd, grad_sib = call(
        grads_kernel,
        [((width, 2 * hid), f32), ((width, 2 * hid), f32), ((2, width, hid), f32)],
        *acts,
        *dpres,
        *after((town, tsib, cown, csib), *firsts),
        scratch=[
            pltpu.VMEM((1024, hid), bf16),
            pltpu.VMEM((1024, hid), bf16),
            pltpu.VMEM((2, width, hid), f32),
            pltpu.SemaphoreType.DMA((2,)),
        ],
        out_spaces=[ANY, ANY, VMEM],
        flops=2 * 2 * 1024 * hid * 2 * width,
    )
    gu, gd = call(
        place_kernel,
        [((width, 2 * hid), f32)] * 2,
        core_swap(grad_sib),
        gu,
        gd,
        scratch=[pltpu.SemaphoreType.DMA((2,))],
        alias={1: 0, 2: 1},
        spaces=[VMEM, ANY, ANY],
        out_spaces=[ANY, ANY],
    )
    lefts[2:] = after(lefts[2:], gu, gd)
    mixed, gtok = call(finish_kernel, [((8, 8, width), bf16)] * 2, *lefts)
    return (mixed.reshape(64, width), gtok.reshape(64, width), gu, gd.T)


def solution(mesh):
    placed = (P("col", "row"), P("row", "col"), P("col", "row"), P("col", "row"))
    return jax.shard_map(
        local,
        mesh=mesh,
        in_specs=placed,
        out_specs=(P("col", "row"), P("col", "row"), P("row", "col"), P("col", "row")),
        check_vma=False,
    )
```

```python
import functools
import math

import jax
import jax.numpy as jnp
from jax import lax
from jax.experimental import pallas as pl
from jax.experimental.pallas import tpu as pltpu
from jax.sharding import PartitionSpec as P

root_coef = math.sqrt(2.0 / math.pi)
f32 = jnp.float32
bf16 = jnp.bfloat16

NZ = 8
NX = 4
NY = 4


def gelu_and_slope(value):
    inner = root_coef * (value + 0.044715 * value * value * value)
    tanh_val = jnp.tanh(inner)
    act = 0.5 * value * (1.0 + tanh_val)
    slope = 0.5 * (1.0 + tanh_val) + 0.5 * value * (1.0 - tanh_val * tanh_val) * root_coef * (
        1.0 + 3.0 * 0.044715 * value * value
    )
    return act, slope


def pairs(axis, which):
    out = []
    size = {"z": NZ, "x": NX, "y": NY}[axis]
    for z in range(NZ):
        for core in range(2):
            for x in range(NX):
                for y in range(NY):
                    at = {"z": z, "x": x, "y": y}
                    step = 1 if (at[axis] + core) % 2 == 0 else -1
                    at[axis] = (at[axis] + {1: step, 2: -step, 3: 2}[which]) % size
                    src = (z * 2 + core) * 16 + x * 4 + y
                    dst = (at["z"] * 2 + core) * 16 + at["x"] * 4 + at["y"]
                    out.append((src, dst))
    return out


PERMS = {
    (axis, which): pairs(axis, which) for axis in "xyz" for which in (1, 2, 3) if axis + str(which) != "z3"
}


def swap(axis, which, value):
    return lax.ppermute(value, ("row", "col"), PERMS[(axis, which)])


def swap1(axis, value):
    return swap(axis, 1, value)


def swap2(axis, value):
    return swap(axis, 2, value)


def core_swap(value):
    return lax.ppermute(value, "row", [(r, r ^ 1) for r in range(2 * NZ)])


def place_of():
    row = lax.axis_index("row")
    z = row // 2
    s = 1 - 2 * ((z + row) & 1)
    return z, s


FLIP = (0, 2, 1, 3)


def stack_kernel(own_ref, one_ref, two_ref, three_ref, tok_ref, cot_ref):
    for x, ref in enumerate((own_ref, one_ref, two_ref, three_ref)):
        tok_ref[x] = ref[0]
        cot_ref[x] = ref[1]


def finish_kernel(mix_own, gtok_own, one_ref, two_ref, three_ref, mix_ref, gtok_ref):
    for i, (own, out) in enumerate(((mix_own, mix_ref), (gtok_own, gtok_ref))):
        total = own[...]
        for ref in (one_ref, two_ref, three_ref):
            total += ref[i].astype(f32)
        out[...] = total.astype(out.dtype)


def token_chunk(owns, sibs, k):
    z, s = place_of()
    at = (z + s * k + 16) & (NZ - 1)
    own, sib = [], []
    for y in range(NY):
        for x in range(NX):
            own.append(owns[y // 2][y % 2, x, at].astype(f32))
            sib.append(sibs[FLIP[y] // 2][FLIP[y] % 2, FLIP[x], at].astype(f32))
    return jnp.concatenate(own, axis=0).astype(bf16), jnp.concatenate(sib, axis=0).astype(bf16)


def far_kernel(*refs, row):
    wown_ref, wsib_ref, part_ref, town_ref, tsib_ref = refs[4:]
    rows = pl.ds(row, town_ref.shape[-1])
    own, sib = token_chunk(refs[:2], refs[2:4], 4)
    town_ref[4] = own
    tsib_ref[4] = sib
    part = jnp.dot(own, wown_ref[rows], preferred_element_type=f32) + jnp.dot(
        sib, wsib_ref[rows], preferred_element_type=f32
    )
    part_ref[...] = part.astype(bf16)


def parts_kernel(*refs, row):
    wown_ref, wsib_ref, _, _, part_ref, town_ref, tsib_ref = refs[4:]
    rows = pl.ds(row, town_ref.shape[-1])
    for k in (3, 5, 2, 6, 1, 7, 0):
        own, sib = token_chunk(refs[:2], refs[2:4], k)
        town_ref[k] = own
        tsib_ref[k] = sib
        part_ref[k] = jnp.dot(own, wown_ref[rows], preferred_element_type=f32) + jnp.dot(
            sib, wsib_ref[rows], preferred_element_type=f32
        )


def outputs_kernel(*refs, ks):
    count = 2 * len(ks)
    wown_ref, wsib_ref = refs[count : count + 2]
    outs = refs[-4:]
    width = outs[0].shape[-1]
    z, s = place_of()
    for i in range(2):
        own_ref, sib_ref = outs[2 * i : 2 * i + 2]
        rows = pl.ds((1 - i) * width, width)
        for chunk, k in zip(refs[i * len(ks) : (i + 1) * len(ks)], ks):
            at = (z + s * k + 16) & (NZ - 1)
            value = chunk[...]
            own = contract_last(value, wown_ref[rows])
            sib = contract_last(value, wsib_ref[rows])
            for y in range(NY):
                for x in range(NX):
                    row = 8 * (y * NX + x)
                    own_ref[y, x, at] = own[row : row + 8]
                    sib_ref[FLIP[y], FLIP[x], at] = sib[row : row + 8].astype(bf16)


def outputs(acts, dpres, weights):
    width = weights[0].shape[0] // 2
    shapes = [((4, 4, 8, 8, width), f32), ((4, 4, 8, 8, width), bf16)] * 2
    flops = 2 * 2 * 128 * weights[0].shape[1] * 2 * width
    most = (0, 1, 7, 2, 6, 3, 5)
    held = call(
        functools.partial(outputs_kernel, ks=most),
        shapes,
        *[chunks[k] for chunks in (acts, dpres) for k in most],
        *weights,
        flops=7 * flops,
    )
    held = call(
        functools.partial(outputs_kernel, ks=(4,)),
        shapes,
        acts[4],
        dpres[4],
        *weights,
        *held,
        alias={4 + i: i for i in range(4)},
        flops=flops,
    )
    return held[:2], held[2:]


def grads_kernel(*refs):
    acts, dpres = refs[:NZ], refs[NZ : 2 * NZ]
    town_ref, tsib_ref, cown_ref, csib_ref, up_ref, down_ref, sib_ref = refs[2 * NZ : 2 * NZ + 7]
    act_ref, dpre_ref, own_ref, sems = refs[2 * NZ + 7 :]
    for k in range(NZ):
        act_ref[128 * k : 128 * k + 128] = acts[k][...]
        dpre_ref[128 * k : 128 * k + 128] = dpres[k][...]
    scale = 1.0 / math.sqrt(1024)
    hid = own_ref.shape[2]
    at = pl.multiple_of((lax.axis_index("row") & 1) * hid, 128)
    sib_ref[0] = contract_first(tsib_ref[...], dpre_ref[...]) * scale
    sib_ref[1] = contract_first(csib_ref[...], act_ref[...]) * scale
    copies = []
    for i, (left, right, out) in enumerate(
        ((town_ref, dpre_ref, up_ref), (cown_ref, act_ref, down_ref))
    ):
        own_ref[i] = contract_first(left[...], right[...]) * scale
        copies.append(
            pltpu.make_async_copy(own_ref.at[i], out.at[:, pl.ds(at, hid)], sems.at[i])
        )
        copies[-1].start()
    for copy in copies:
        copy.wait()


def place_kernel(sib_ref, up_in, down_in, up_ref, down_ref, sems):
    hid = sib_ref.shape[2]
    at = pl.multiple_of((1 - (lax.axis_index("row") & 1)) * hid, 128)
    copies = [
        pltpu.make_async_copy(sib_ref.at[i], out.at[:, pl.ds(at, hid)], sems.at[i])
        for i, out in enumerate((up_ref, down_ref))
    ]
    for copy in copies:
        copy.start()
    for copy in copies:
        copy.wait()


VMEM = pl.BlockSpec(memory_space=pltpu.VMEM)


def call(kernel, outs, *args, scratch=(), flops=0, alias=None, spaces=None, out_spaces=None):
    return pl.pallas_call(
        kernel,
        out_shape=[jax.ShapeDtypeStruct(shape, dtype) for shape, dtype in outs],
        in_specs=spaces or [VMEM] * len(args),
        out_specs=out_spaces or [VMEM] * len(outs),
        scratch_shapes=list(scratch),
        input_output_aliases=alias or {},
        compiler_params=pltpu.CompilerParams(vmem_limit_bytes=16 * 1024 * 1024),
        cost_estimate=pl.CostEstimate(flops=flops, bytes_accessed=4 << 20, transcendentals=0),
    )(*args)


ANY = pl.BlockSpec(memory_space=pl.ANY)


def gather_tokens(block):
    got = [swap("x", which, block) for which in (1, 2, 3)]
    shape = (4,) + block.shape[1:]
    both = call(stack_kernel, [(shape, bf16)] * 2, block, *got)
    near = [jnp.stack([held, swap1("y", held)]) for held in both]
    far = [swap2("y", held) for held in near]
    near_sib = [core_swap(held) for held in near]
    return got[0], [(near[i], far[i], near_sib[i], core_swap(far[i])) for i in range(2)]


def reduce_tokens(pairs):
    last, moving, firsts, second = (), [], [], None
    for own, sib in pairs:
        part = own + after(core_swap(sib), *last).astype(f32)
        sent = part[2:].astype(bf16)
        last = (sent,)
        firsts.append(sent)
        moving.append((part[:2], swap2("y", sent)))
    for i, (keep, got) in enumerate(moving):
        part = keep + after(got, *last).astype(f32)
        sent = part[1].astype(bf16)
        last = (sent,)
        second = sent if i == 0 else second
        moving[i] = (part[0], swap1("y", sent))
    parts = [keep + after(got, *last).astype(f32) for keep, got in moving]
    sent, last = [], ()
    for which in (3, 2, 1):
        pair = after([part[which] for part in parts], *last)
        sent.append(jnp.stack(pair).astype(bf16))
        last = (sent[-1],)
    lefts = [swap("x", 3 - i, value) for i, value in enumerate(sent)]
    return [part[0] for part in parts] + lefts, firsts, second


def after(values, *earlier):
    held = lax.optimization_barrier((values, earlier))
    return held[0]


TURNS = (((0, 1), (1, 2), (0, 2), (1, 1)), ((0, 2), (1, 1), (0, 1), (1, 2)))


def reduce_z(firsts, parts):
    last = ()
    got = {(0, 1): swap1("z", firsts[0]), (1, 2): swap2("z", firsts[1])}
    for k in (3, 2, 1):
        sent = {}
        for i, way in (TURNS[(3 - k) % 2] if k > 1 else ((0, 1), (0, 2), (1, 2), (1, 1))):
            part = parts[i][k if way == 1 else 8 - k]
            if (i, 3 - way) in got:
                part = part + after(got[(i, 3 - way)], *last).astype(f32)
            part = part.astype(bf16)
            last = (part,)
            sent[(i, way)] = swap("z", way, part)
        got = sent
    sums = []
    for i, part in enumerate(parts):
        first, second = after((got[(i, 1)], got[(i, 2)]), *last)
        sums.append(part[0] + first.astype(f32) + second.astype(f32))
        last = (sums[-1],)
    return sums


def gather_z(owns):
    gots = [{0: own} for own in owns]
    for i, way in TURNS[0]:
        gots[i][1 if way == 1 else 7] = swap("z", way, owns[i])
    last = ()
    for k in (2, 3, 4):
        for i, way in TURNS[(k - 1) % 2]:
            got = gots[i]
            at = 9 - k if way == 1 else k - 1
            got[at] = after(got[at], *last)
            last = (got[at],)
            if k < 4:
                got[k if way == 1 else 8 - k] = swap("z", way, got[at])
            elif way == 2 - i:
                got[4] = swap("z", way, got[at])
    return [[got[k] for k in range(8)] for got in gots]


def contract_last(left, right):
    return lax.dot_general(left, right, (((1,), (1,)), ((), ())), preferred_element_type=f32)


def contract_first(left, right):
    return lax.dot_general(left, right, (((0,), (0,)), ((), ())), preferred_element_type=f32)


def local(tokens, up_weight, down_weight, cotangent):
    core = lax.axis_index("row") % 2
    width = tokens.shape[1]
    hid = up_weight.shape[1] // 2

    block = jnp.stack([tokens.reshape(8, 8, width), cotangent.reshape(8, 8, width)])
    first, (tok_parts, cot_parts) = gather_tokens(block)

    up_weight, down_weight = after((up_weight, down_weight), first)
    weights = jnp.concatenate([up_weight, down_weight.T], axis=0)
    wown = lax.dynamic_slice_in_dim(weights, core * hid, hid, 1)
    wsib = core_swap(lax.dynamic_slice_in_dim(weights, (1 - core) * hid, hid, 1))

    def far(pieces, row):
        return call(
            functools.partial(far_kernel, row=row),
            [((128, hid), bf16)] + [((8, 128, width), bf16)] * 2,
            *pieces,
            wown,
            wsib,
            flops=2 * 128 * hid * 2 * width,
        )

    def parts(pieces, row, town, tsib):
        out = call(
            functools.partial(parts_kernel, row=row),
            [((8, 128, hid), f32), ((8, 128, width), bf16), ((8, 128, width), bf16)],
            *pieces,
            *after((wown, wsib), *sends),
            town,
            tsib,
            alias={6: 1, 7: 2},
            flops=2 * 1024 * hid * 2 * width,
        )
        return out[0], out[1].reshape(1024, width), out[2].reshape(1024, width)

    tok_far, town, tsib = far(tok_parts, 0)
    cot_far, cown, csib = far(cot_parts, width)
    sends = (tok_far, cot_far)
    pre_part, town, tsib = parts(tok_parts, 0, town, tsib)
    dact_part, cown, csib = parts(cot_parts, width, cown, csib)
    pre, dact = reduce_z([tok_far, cot_far], [pre_part, dact_part])
    act, slope = gelu_and_slope(pre)
    acts, dpres = gather_z([act.astype(bf16), (dact * slope).astype(bf16)])

    pairs = outputs(acts, dpres, (wown, wsib))
    lefts, firsts, second = reduce_tokens(pairs)
    gu, gd, grad_sib = call(
        grads_kernel,
        [((width, 2 * hid), f32), ((width, 2 * hid), f32), ((2, width, hid), f32)],
        *acts,
        *dpres,
        *after((town, tsib, cown, csib), *firsts),
        scratch=[
            pltpu.VMEM((1024, hid), bf16),
            pltpu.VMEM((1024, hid), bf16),
            pltpu.VMEM((2, width, hid), f32),
            pltpu.SemaphoreType.DMA((2,)),
        ],
        out_spaces=[ANY, ANY, VMEM],
        flops=2 * 2 * 1024 * hid * 2 * width,
    )
    gu, gd = call(
        place_kernel,
        [((width, 2 * hid), f32)] * 2,
        core_swap(after(grad_sib, second)),
        gu,
        gd,
        scratch=[pltpu.SemaphoreType.DMA((2,))],
        alias={1: 0, 2: 1},
        spaces=[VMEM, ANY, ANY],
        out_spaces=[ANY, ANY],
    )
    lefts[2:] = after(lefts[2:], gu, gd)
    mixed, gtok = call(finish_kernel, [((8, 8, width), bf16)] * 2, *lefts)
    return (mixed.reshape(64, width), gtok.reshape(64, width), gu, gd.T)


def solution(mesh):
    placed = (P("col", "row"), P("row", "col"), P("col", "row"), P("col", "row"))
    return jax.shard_map(
        local,
        mesh=mesh,
        in_specs=placed,
        out_specs=(P("col", "row"), P("col", "row"), P("row", "col"), P("col", "row")),
        check_vma=False,
    )
```
